128 devices in a mesh: gx: 4 (over y_hi, core), gy: 4 (over z), gz: 8 (over y_lo, x).
Axes of the slice: x: 4, y: 4 (y_hi: 2, y_lo: 2; y = y_hi * 2 + y_lo), z: 4, core: 2. Of those that a mesh axis runs over, the one named last changes fastest.
Arguments:
- block_in: bfloat16 [768, 8192], P(('gy', 'gz'), 'gx'), may hold values from -6 to 6
- online_gate: bfloat16 [8192, 16384], P('gx', ('gy', 'gz')), may hold values from -6 to 6
- online_up: bfloat16 [8192, 16384], P('gx', ('gy', 'gz')), may hold values from -6 to 6
- online_down: bfloat16 [16384, 8192], P(('gy', 'gz'), 'gx'), may hold values from -6 to 6
- target_gate: bfloat16 [8192, 16384], P('gx', ('gy', 'gz')), may hold values from -6 to 6
- target_up: bfloat16 [8192, 16384], P('gx', ('gy', 'gz')), may hold values from -6 to 6
- target_down: bfloat16 [16384, 8192], P(('gy', 'gz'), 'gx'), may hold values from -6 to 6
- cotangent: bfloat16 [768, 8192], P(('gy', 'gz'), 'gx'), may hold values from -6 to 6
Outputs:
- online_out: bfloat16 [768, 8192], P(('gy', 'gz'), 'gx')
- target_out: bfloat16 [768, 8192], P(('gy', 'gz'), 'gx')
- grad_in: bfloat16 [768, 8192], P(('gy', 'gz'), 'gx')
- grad_gate: bfloat16 [8192, 16384], P('gx', ('gy', 'gz'))
- grad_up: bfloat16 [8192, 16384], P('gx', ('gy', 'gz'))
- grad_down: bfloat16 [16384, 8192], P(('gy', 'gz'), 'gx')
- new_gate: bfloat16 [8192, 16384], P('gx', ('gy', 'gz'))
- new_up: bfloat16 [8192, 16384], P('gx', ('gy', 'gz'))
- new_down: bfloat16 [16384, 8192], P(('gy', 'gz'), 'gx')
The draws below stay inside these ranges and needn't reach their ends.
All inputs are finite; a program needn't handle non-finite values.
Results may differ from the reference program's by a relative error of at most 0.0049.
Values may be sent and summed in bfloat16 or wider, within the bound.
No kernel may reach another device: no remote copies, remote signals or barrier semaphores. Data moves between devices by JAX's collectives and lax.ppermute only.
A program may use at most 128 MiB of HBM per device.

```python
import math
import jax
import jax.numpy as jnp

D = 8192
FF = 16384
TOKENS = 768


def block_levels(own_key, extent, pieces, low, high):
    level = 1.0
    for position, parts in pieces:
        steps = jax.random.uniform(jax.random.fold_in(jax.random.fold_in(own_key, 6), position), (parts,), jnp.float32, low / len(pieces), high / len(pieces))
        level = level * jnp.repeat(jnp.exp(steps), extent[position] // parts).reshape((-1,) + (1,) * (len(extent) - 1 - position))
    return level


def centred(key, shape, scale, bound, shards=(), kind=jnp.bfloat16):
    values = scale * jax.random.normal(key, shape, jnp.float32)
    if shards:
        values = values * block_levels(key, shape, shards, -0.22, 0.18)
    return jnp.clip(values, -bound, bound).astype(kind)


def setup_inputs(seed: int = 0) -> dict:
    streams_of = jax.random.split(jax.random.key(seed), 9)
    return {
        "block_in": centred(streams_of[0], (TOKENS, D), 1.0, 6.0, ((0, 32), (1, 4))),
        "online_gate": centred(streams_of[1], (D, FF), 1.0, 6.0, ((0, 4), (1, 32))),
        "online_up": centred(streams_of[2], (D, FF), 1.0, 6.0, ((0, 4), (1, 32))),
        "online_down": centred(streams_of[3], (FF, D), 1.0, 6.0, ((0, 32), (1, 4))),
        "target_gate": centred(streams_of[4], (D, FF), 1.0, 6.0, ((0, 4), (1, 32))),
        "target_up": centred(streams_of[5], (D, FF), 1.0, 6.0, ((0, 4), (1, 32))),
        "target_down": centred(streams_of[6], (FF, D), 1.0, 6.0, ((0, 32), (1, 4))),
        "cotangent": centred(streams_of[7], (TOKENS, D), 1.0, 6.0, ((0, 32), (1, 4))),
    }


POLYAK = 0.05

def swiglu_parts(block_in, weight_gate, weight_up):
    scale_in = 1.0 / math.sqrt(D)
    pre_gate = jnp.dot(block_in, weight_gate, preferred_element_type=jnp.float32) * scale_in
    pre_up = jnp.dot(block_in, weight_up, preferred_element_type=jnp.float32) * scale_in
    hidden = (jax.nn.silu(pre_gate) * pre_up).astype(jnp.bfloat16)
    return (pre_gate, pre_up, hidden)

def blend(online, target):
    online_f = online.astype(jnp.float32)
    target_f = target.astype(jnp.float32)
    return (target_f + POLYAK * (online_f - target_f)).astype(jnp.bfloat16)

def reference(block_in, online_gate, online_up, online_down, target_gate, target_up, target_down, cotangent):
    scale_in = 1.0 / math.sqrt(D)
    scale_hid = 1.0 / math.sqrt(FF)
    on_gate, on_up, on_hidden = swiglu_parts(block_in, online_gate, online_up)
    _, _, tg_hidden = swiglu_parts(block_in, target_gate, target_up)
    online_out = (jnp.dot(on_hidden, online_down, preferred_element_type=jnp.float32) * scale_hid).astype(jnp.bfloat16)
    target_out = (jnp.dot(tg_hidden, target_down, preferred_element_type=jnp.float32) * scale_hid).astype(jnp.bfloat16)
    hidden_grad = jnp.dot(cotangent, online_down.T, preferred_element_type=jnp.float32) * scale_hid
    sigmoid_value = jax.nn.sigmoid(on_gate)
    d_up = (hidden_grad * on_gate * sigmoid_value).astype(jnp.bfloat16)
    d_gate = (hidden_grad * on_up * sigmoid_value * (1.0 + on_gate * (1.0 - sigmoid_value))).astype(jnp.bfloat16)
    summed = jnp.dot(d_gate, online_gate.T, preferred_element_type=jnp.float32)
    summed = summed + jnp.dot(d_up, online_up.T, preferred_element_type=jnp.float32)
    grad_in = (summed * scale_in).astype(jnp.bfloat16)
    grad_gate = (jnp.dot(block_in.T, d_gate, preferred_element_type=jnp.float32) * scale_in).astype(jnp.bfloat16)
    grad_up = (jnp.dot(block_in.T, d_up, preferred_element_type=jnp.float32) * scale_in).astype(jnp.bfloat16)
    grad_down = (jnp.dot(on_hidden.T, cotangent, preferred_element_type=jnp.float32) * scale_hid).astype(jnp.bfloat16)
    new_gate = blend(online_gate, target_gate)
    new_up = blend(online_up, target_up)
    new_down = blend(online_down, target_down)
    return (online_out, target_out, grad_in, grad_gate, grad_up, grad_down, new_gate, new_up, new_down)
```

```python
import math

import jax
import jax.numpy as jnp
from jax import lax
from jax.sharding import PartitionSpec as P

D = 8192
FF = 16384
POLYAK = 0.05
TOKENS = ("gy", "gz")
BF = jnp.bfloat16
F32 = jnp.float32


def activate(pre_gate, pre_up):
    return (jax.nn.silu(pre_gate) * pre_up).astype(BF)


def hidden_grads(pre_gate, pre_up, hidden_grad):
    sigmoid_value = jax.nn.sigmoid(pre_gate)
    d_up = (hidden_grad * pre_gate * sigmoid_value).astype(BF)
    d_gate = (
        hidden_grad * pre_up * sigmoid_value * (1.0 + pre_gate * (1.0 - sigmoid_value))
    ).astype(BF)
    return (d_gate, d_up)


def blend(online, target):
    online_f = online.astype(F32)
    target_f = target.astype(F32)
    return (target_f + POLYAK * (online_f - target_f)).astype(BF)


def gather_rows(rows):
    copies = jnp.broadcast_to(rows[None], (32,) + rows.shape)
    got = lax.all_to_all(copies, TOKENS, 0, 0)
    return got.reshape(32 * rows.shape[0], rows.shape[1])


def scatter_sum(part):
    chunks = part.reshape(32, part.shape[0] // 32, part.shape[1])
    got = lax.all_to_all(chunks, TOKENS, 0, 0)
    return jnp.sum(got.astype(F32), axis=0).astype(BF)


def other_core(value):
    return lax.ppermute(value, "gx", [(0, 1), (1, 0), (2, 3), (3, 2)])


def other_half(value):
    return lax.ppermute(value, "gx", [(0, 2), (1, 3), (2, 0), (3, 1)])


def on_device(
    block_in, online_gate, online_up, online_down, target_gate, target_up, target_down, cotangent
):
    scale_in = 1.0 / math.sqrt(D)
    scale_hid = 1.0 / math.sqrt(FF)
    core = lax.axis_index("gx") % 2
    rows_all = gather_rows(block_in)
    cot_all = gather_rows(cotangent)

    def halves(value):
        half = value.shape[0] // 2
        keep = lax.dynamic_slice_in_dim(value, core * half, half, 0)
        send = lax.dynamic_slice_in_dim(value, (1 - core) * half, half, 0)
        return keep, send

    def width_sum(keep, send):
        chip = keep + other_core(send).astype(F32)
        return chip + other_half(chip.astype(BF)).astype(F32)

    def both_halves(value):
        other = other_core(value)
        lower = jnp.where(core == 0, value, other)
        upper = jnp.where(core == 0, other, value)
        return jnp.concatenate([lower, upper], axis=0)

    rows_keep, rows_send = halves(rows_all)

    def project(gate, up):
        def both(rows):
            return jnp.concatenate(
                [
                    jnp.dot(rows, gate, preferred_element_type=F32) * scale_in,
                    jnp.dot(rows, up, preferred_element_type=F32) * scale_in,
                ],
                axis=1,
            )

        pre = width_sum(both(rows_keep), both(rows_send).astype(BF))
        return pre[:, :512], pre[:, 512:]

    tg_gate, tg_up = project(target_gate, target_up)
    on_gate, on_up = project(online_gate, online_up)
    tg_hidden = both_halves(activate(tg_gate, tg_up))
    target_out = scatter_sum(
        (jnp.dot(tg_hidden, target_down, preferred_element_type=F32) * scale_hid).astype(BF)
    )
    cot_keep, cot_send = halves(cot_all)

    def back(rows):
        return jnp.einsum("tk,fk->tf", rows, online_down, preferred_element_type=F32) * scale_hid

    hidden_grad = width_sum(back(cot_keep), back(cot_send).astype(BF))
    d_gate, d_up = hidden_grads(on_gate, on_up, hidden_grad)
    packed = both_halves(jnp.concatenate([activate(on_gate, on_up), d_gate, d_up], axis=1))
    on_hidden, d_gate, d_up = packed[:, :512], packed[:, 512:1024], packed[:, 1024:]
    online_out = scatter_sum(
        (jnp.dot(on_hidden, online_down, preferred_element_type=F32) * scale_hid).astype(BF)
    )
    summed = jnp.einsum("tf,kf->tk", d_gate, online_gate, preferred_element_type=F32)
    summed = summed + jnp.einsum("tf,kf->tk", d_up, online_up, preferred_element_type=F32)
    grad_in = scatter_sum((summed * scale_in).astype(BF))
    grad_gate = (
        jnp.einsum("tk,tf->kf", rows_all, d_gate, preferred_element_type=F32) * scale_in
    ).astype(BF)
    grad_up = (
        jnp.einsum("tk,tf->kf", rows_all, d_up, preferred_element_type=F32) * scale_in
    ).astype(BF)
    grad_down = (
        jnp.einsum("tf,tk->fk", on_hidden, cot_all, preferred_element_type=F32) * scale_hid
    ).astype(BF)
    new_gate = blend(online_gate, target_gate)
    new_up = blend(online_up, target_up)
    new_down = blend(online_down, target_down)
    return (
        online_out,
        target_out,
        grad_in,
        grad_gate,
        grad_up,
        grad_down,
        new_gate,
        new_up,
        new_down,
    )


def solution(mesh):
    tokens = P(("gy", "gz"), "gx")
    wide = P("gx", ("gy", "gz"))
    tall = P(("gy", "gz"), "gx")
    return jax.shard_map(
        on_device,
        mesh=mesh,
        in_specs=(tokens, wide, wide, tall, wide, wide, tall, tokens),
        out_specs=(tokens, tokens, tokens, wide, wide, tall, wide, wide, tall),
        check_vma=False,
    )
```

```python
import math

import jax
import jax.numpy as jnp
from jax import lax
from jax.sharding import PartitionSpec as P

D = 8192
FF = 16384
POLYAK = 0.05
BF = jnp.bfloat16
F32 = jnp.float32
SCALE_IN = 1.0 / math.sqrt(D)
SCALE_HID = 1.0 / math.sqrt(FF)
FAR = (0, 1, 3, 2)


def activate(pre_gate, pre_up):
    return (jax.nn.silu(pre_gate) * pre_up).astype(BF)


def hidden_grads(pre_gate, pre_up, hidden_grad):
    sigmoid_value = jax.nn.sigmoid(pre_gate)
    d_up = (hidden_grad * pre_gate * sigmoid_value).astype(BF)
    d_gate = (
        hidden_grad * pre_up * sigmoid_value * (1.0 + pre_gate * (1.0 - sigmoid_value))
    ).astype(BF)
    return (d_gate, d_up)


def blend(online, target):
    online_f = online.astype(F32)
    target_f = target.astype(F32)
    return (target_f + POLYAK * (online_f - target_f)).astype(BF)


def shifted(value, dz, dy, dx):
    pairs = []
    for z in range(4):
        for y in range(2):
            for x in range(4):
                to = ((z + dz) % 4 * 2 + (y + dy) % 2) * 4 + (x + dx) % 4
                pairs.append(((z * 2 + y) * 4 + x, to))
    return lax.ppermute(value, ("gy", "gz"), pairs)


def along_x(value, d):
    return shifted(value, 0, 0, d)


def along_z(value, d):
    return shifted(value, d, 0, 0)


def swap_zx(value):
    rows, columns = value.shape
    return value.reshape(4, 4, rows // 16, columns).swapaxes(0, 1).reshape(rows, columns)


def from_axis(value, along):
    return [value] + [along(value, d) for d in FAR[1:]]


def to_axis(parts, along):
    return [parts[0]] + [along(part, -d) for part, d in list(zip(parts, FAR))[1:]]


def total_of(parts):
    total = parts[0].astype(F32)
    for part in parts[1:]:
        total = total + part.astype(F32)
    return total


def stack(parts):
    return jnp.concatenate(list(parts), axis=0)


def beside(parts):
    return jnp.concatenate(list(parts), axis=1)


def split(value):
    return jnp.split(value, 4, axis=0)


def other_core(value):
    return lax.ppermute(value, "gx", [(0, 1), (1, 0), (2, 3), (3, 2)])


def other_half(value):
    return lax.ppermute(value, "gx", [(0, 2), (1, 3), (2, 0), (3, 1)])


def after(value, *others):
    return lax.optimization_barrier((value,) + others)[0]


def together(*values):
    return lax.optimization_barrier(values)


def on_device(
    block_in, online_gate, online_up, online_down, target_gate, target_up, target_down, cotangent
):
    core = lax.axis_index("gx") % 2

    def halves(value):
        half = value.shape[0] // 2
        keep = lax.dynamic_slice_in_dim(value, core * half, half, 0)
        send = lax.dynamic_slice_in_dim(value, (1 - core) * half, half, 0)
        return keep, send

    def both_halves(value):
        other = other_core(value)
        lower = jnp.where(core == 0, value, other)
        upper = jnp.where(core == 0, other, value)
        return stack([lower, upper])

    def project(rows, weight):
        return jnp.dot(rows, weight, preferred_element_type=F32) * SCALE_IN

    def back(rows):
        return jnp.einsum("tk,fk->tf", rows, online_down, preferred_element_type=F32) * SCALE_HID

    def down(hidden, weight):
        return (jnp.dot(hidden, weight, preferred_element_type=F32) * SCALE_HID).astype(BF)

    pair = shifted(stack([block_in, cotangent]), 0, 1, 0)
    rows = stack([block_in, pair[:24]])
    cot = stack([cotangent, pair[24:]])
    left = stack(from_axis(rows[:, :1024], along_x))
    right = stack(from_axis(rows[:, 1024:], along_z))
    left = stack(from_axis(left, along_z))
    right = stack(from_axis(right, along_x))
    rows_all = beside([left, swap_zx(right)])

    rows_keep, rows_send = halves(rows_all)
    tg_send = beside([project(rows_send, w) for w in (target_gate, target_up)])
    on_send = beside([project(rows_send, w) for w in (online_gate, online_up)])
    tg_got = other_core(tg_send)
    on_send, cot = together(on_send, cot)
    on_got = other_core(on_send)
    cot = from_axis(cot, along_x)
    tg_keep = beside([project(rows_keep, w) for w in (target_gate, target_up)])
    on_keep = beside([project(rows_keep, w) for w in (online_gate, online_up)])
    tg_keep, on_keep, tg_got, on_got, cot = together(tg_keep, on_keep, tg_got, on_got, cot)
    tg_chip = tg_keep + tg_got
    on_chip = on_keep + on_got
    wire, cot = together(beside([tg_chip.astype(BF), on_chip.astype(BF)]), stack(cot))
    there = other_half(wire)
    cot = from_axis(cot, along_z)
    old_gate, old_up, old_down = after((target_gate, target_up, target_down), cot[1], cot[3])
    blends = (
        blend(online_gate, old_gate), blend(online_up, old_up), blend(online_down, old_down)
    )
    there, cot, (new_gate, new_up, new_down) = together(there, cot, blends)

    cot_all = stack(cot)
    cot_keep, cot_send = halves(cot_all)
    back_got = other_core(back(cot_send))
    back_chip = back(cot_keep) + back_got
    back_wire = back_chip.astype(BF)
    back_there = other_half(back_wire)
    there = after(there, back_wire)

    tg_pre = tg_chip + there[:, :1024].astype(F32)
    on_pre = on_chip + there[:, 1024:].astype(F32)
    on_gate, on_up = on_pre[:, :512], on_pre[:, 512:]
    hidden = both_halves(
        beside([activate(tg_pre[:, :512], tg_pre[:, 512:]), activate(on_gate, on_up)])
    )
    tg_hidden, on_hidden = hidden[:, :512], hidden[:, 512:]

    tg_parts = split(down(tg_hidden, target_down))
    on_parts = split(down(swap_zx(on_hidden), online_down))
    tg_parts, on_parts = together(tg_parts, on_parts)
    tg_far = to_axis(tg_parts, along_z)
    on_far = to_axis(on_parts, along_x)

    back_there = after(back_there, tg_far[1], on_far[1])
    hidden_grad = back_chip + back_there.astype(F32)
    grads = both_halves(beside(hidden_grads(on_gate, on_up, hidden_grad)))

    def inward(grads, half):
        rows = slice(1024 * half, 1024 * half + 1024)
        summed = jnp.einsum(
            "tf,kf->tk", grads[:, :512], online_gate[rows], preferred_element_type=F32
        )
        summed = summed + jnp.einsum(
            "tf,kf->tk", grads[:, 512:], online_up[rows], preferred_element_type=F32
        )
        return (summed * SCALE_IN).astype(BF)

    left_parts = split(inward(grads, 0))
    right_parts = split(inward(swap_zx(grads), 1))
    left_parts, right_parts = together(left_parts, right_parts)
    left_far = to_axis(left_parts, along_z)
    right_far = to_axis(right_parts, along_x)

    late_rows, late_cot = after((rows_all, cot_all), left_parts, tg_far[1], on_far[1])
    d_gate, d_up = grads[:, :512], grads[:, 512:]
    grad_gate = (
        jnp.einsum("tk,tf->kf", late_rows, d_gate, preferred_element_type=F32) * SCALE_IN
    ).astype(BF)
    grad_up = (
        jnp.einsum("tk,tf->kf", late_rows, d_up, preferred_element_type=F32) * SCALE_IN
    ).astype(BF)
    grad_down = (
        jnp.einsum("tf,tk->fk", on_hidden, late_cot, preferred_element_type=F32) * SCALE_HID
    ).astype(BF)
    tg_far, on_far, left_far, right_far, weight_grads = together(
        tg_far, on_far, left_far, right_far, (grad_gate, grad_up, grad_down)
    )
    grad_gate, grad_up, grad_down = weight_grads

    def near(first, second, along):
        sums = [total_of(first).astype(BF), total_of(second).astype(BF)]
        return total_of(to_axis(split(beside(sums)), along))

    left = near(tg_far, left_far, along_x)
    right = near(on_far, right_far, along_z)
    total = beside([left, right])
    total = (total[:24] + shifted(total[24:], 0, 1, 0)).astype(BF)
    target_out, online_out = total[:, :2048], total[:, 3072:5120]
    grad_in = beside([total[:, 2048:3072], total[:, 5120:]])
    return (
        online_out,
        target_out,
        grad_in,
        grad_gate,
        grad_up,
        grad_down,
        new_gate,
        new_up,
        new_down,
    )


def solution(mesh):
    tokens = P(("gy", "gz"), "gx")
    wide = P("gx", ("gy", "gz"))
    tall = P(("gy", "gz"), "gx")
    return jax.shard_map(
        on_device,
        mesh=mesh,
        in_specs=(tokens, wide, wide, tall, wide, wide, tall, tokens),
        out_specs=(tokens, tokens, tokens, wide, wide, tall, wide, wide, tall),
        check_vma=False,
    )
```

```python
import math

import jax
import jax.numpy as jnp
from jax import lax
from jax.sharding import PartitionSpec as P

D = 8192
FF = 16384
POLYAK = 0.05
BF = jnp.bfloat16
F32 = jnp.float32
SCALE_IN = 1.0 / math.sqrt(D)
SCALE_HID = 1.0 / math.sqrt(FF)
FAR = (0, 1, 3, 2)


def activate(pre_gate, pre_up):
    return (jax.nn.silu(pre_gate) * pre_up).astype(BF)


def hidden_grads(pre_gate, pre_up, hidden_grad):
    sigmoid_value = jax.nn.sigmoid(pre_gate)
    d_up = (hidden_grad * pre_gate * sigmoid_value).astype(BF)
    d_gate = (
        hidden_grad * pre_up * sigmoid_value * (1.0 + pre_gate * (1.0 - sigmoid_value))
    ).astype(BF)
    return (d_gate, d_up)


def blend(online, target):
    online_f = online.astype(F32)
    target_f = target.astype(F32)
    return (target_f + POLYAK * (online_f - target_f)).astype(BF)


def shifted(value, dz, dy, dx):
    pairs = []
    for z in range(4):
        for y in range(2):
            for x in range(4):
                to = ((z + dz) % 4 * 2 + (y + dy) % 2) * 4 + (x + dx) % 4
                pairs.append(((z * 2 + y) * 4 + x, to))
    return lax.ppermute(value, ("gy", "gz"), pairs)


def along_x(value, d):
    return shifted(value, 0, 0, d)


def along_z(value, d):
    return shifted(value, d, 0, 0)


def swap_zx(value):
    rows, columns = value.shape
    return value.reshape(4, 4, rows // 16, columns).swapaxes(0, 1).reshape(rows, columns)


def from_axis(value, along):
    return [value] + [along(value, d) for d in FAR[1:]]


def together(*values):
    return lax.optimization_barrier(values)


def passed_on(near, along):
    half = near[0].shape[0] // 2
    return [along(near[0][:half], 1), along(near[1][half:], 3)]


def halves_out(parts, along):
    far = parts[-1]
    half = far.shape[0] // 2
    return [along(far[:half], -1), along(far[half:], 1)]


def with_passing(parts, passing):
    _, back, ahead, _ = parts
    half = back.shape[0] // 2
    back = [(back[:half].astype(F32) + passing[0].astype(F32)).astype(BF), back[half:]]
    ahead = [ahead[:half], (ahead[half:].astype(F32) + passing[1].astype(F32)).astype(BF)]
    return [stack(back), stack(ahead)]


def to_axis(parts, along):
    return [parts[0]] + [along(part, -d) for part, d in list(zip(parts, FAR))[1:]]


def total_of(parts):
    total = parts[0].astype(F32)
    for part in parts[1:]:
        total = total + part.astype(F32)
    return total


def stack(parts):
    return jnp.concatenate(list(parts), axis=0)


def beside(parts):
    return jnp.concatenate(list(parts), axis=1)


def split(value):
    return jnp.split(value, 4, axis=0)


def other_core(value):
    return lax.ppermute(value, "gx", [(0, 1), (1, 0), (2, 3), (3, 2)])


def other_half(value):
    return lax.ppermute(value, "gx", [(0, 2), (1, 3), (2, 0), (3, 1)])


def after(value, *others):
    return lax.optimization_barrier((value,) + others)[0]


def on_device(
    block_in, online_gate, online_up, online_down, target_gate, target_up, target_down, cotangent
):
    core = lax.axis_index("gx") % 2

    def halves(value):
        half = value.shape[0] // 2
        keep = lax.dynamic_slice_in_dim(value, core * half, half, 0)
        send = lax.dynamic_slice_in_dim(value, (1 - core) * half, half, 0)
        return keep, send

    def both_halves(value):
        other = other_core(value)
        lower = jnp.where(core == 0, value, other)
        upper = jnp.where(core == 0, other, value)
        return stack([lower, upper])

    def project(rows, weight):
        return jnp.dot(rows, weight, preferred_element_type=F32) * SCALE_IN

    def back(rows):
        return jnp.einsum("tk,fk->tf", rows, online_down, preferred_element_type=F32) * SCALE_HID

    def down(hidden, weight):
        return (jnp.dot(hidden, weight, preferred_element_type=F32) * SCALE_HID).astype(BF)

    def outward(whole, gate, up):
        summed = jnp.einsum("tf,kf->tk", whole[:, :512], gate, preferred_element_type=F32)
        summed = summed + jnp.einsum("tf,kf->tk", whole[:, 512:], up, preferred_element_type=F32)
        return (summed * SCALE_IN).astype(BF)

    own = stack([block_in, cotangent])
    pair = shifted(own, 0, 1, 0)
    pair = beside([stack([own[:24], pair[:24]]), stack([own[24:], pair[24:]])])
    left = beside([pair[:, :1024], pair[:, 2048:3072]])
    right = beside([pair[:, 1024:2048], pair[:, 3072:]])
    left, right = together(left, right)
    left, right = together(from_axis(left, along_x), from_axis(right, along_z))
    left, right = together(stack(left), stack(right))
    left_near = [along_z(left, 1), along_z(left, 3)]
    right_near = [along_x(right, 1), along_x(right, 3)]
    old_gate, old_up = after((target_gate, target_up), left, right)
    blends = (blend(online_gate, old_gate), blend(online_up, old_up))
    left_near, right_near, (new_gate, new_up) = together(left_near, right_near, blends)
    left = [left] + left_near + passed_on(left_near, along_z)
    right = [right] + right_near + passed_on(right_near, along_x)
    left, right = stack(left), swap_zx(stack(right))
    rows_all = beside([left[:, :1024], right[:, :1024]])
    cot_all = beside([left[:, 1024:], right[:, 1024:]])

    rows_keep, rows_send = halves(rows_all)
    tg_send = beside([project(rows_send, w) for w in (target_gate, target_up)])
    tg_got = other_core(tg_send)
    tg_keep = beside([project(rows_keep, w) for w in (target_gate, target_up)])
    cot_late, rows_late = after((cot_all, rows_all), tg_keep)
    cot_keep, cot_send = halves(cot_late)
    rows_keep, rows_send = halves(rows_late)
    on_got = other_core(beside([project(rows_send, w) for w in (online_gate, online_up)]))
    back_got = other_core(back(cot_send))
    tg_chip = tg_keep + tg_got
    tg_wire, rows_keep, cot_keep = together(tg_chip.astype(BF), rows_keep, cot_keep)
    tg_there = other_half(tg_wire)
    on_chip = beside([project(rows_keep, w) for w in (online_gate, online_up)]) + on_got
    back_chip = back(cot_keep) + back_got
    wire = beside([on_chip, back_chip]).astype(BF)
    tg_there, wire = together(tg_there, wire)
    there = other_half(wire)

    pre = tg_chip + tg_there.astype(F32)
    hidden = both_halves(activate(pre[:, :512], pre[:, 512:]))
    tg_left = split(down(hidden, target_down[:, :1024]))
    tg_right = split(down(swap_zx(hidden), target_down[:, 1024:]))
    tg_left[1:3] = [along_z(tg_left[1], -1), along_z(tg_left[2], 1)]
    tg_right[1:3] = [along_x(tg_right[1], -1), along_x(tg_right[2], 1)]
    tg_left[3] = along_z(after(tg_left[3], tg_left[1]), 2)
    tg_right[3] = along_x(after(tg_right[3], tg_right[1]), 2)
    there, tg_left, tg_right = together(there, tg_left, tg_right)

    pre = on_chip + there[:, :1024].astype(F32)
    on_gate, on_up = pre[:, :512], pre[:, 512:]
    hidden_grad = back_chip + there[:, 1024:].astype(F32)
    d_gate, d_up = hidden_grads(on_gate, on_up, hidden_grad)
    whole = both_halves(beside([activate(on_gate, on_up), d_gate, d_up]))
    swapped = swap_zx(whole)

    def left_terms(rows):
        return beside(
            [
                down(rows[:, :512], online_down[:, :1024]),
                outward(rows[:, 512:], online_gate[:1024], online_up[:1024]),
            ]
        )

    def right_terms(rows):
        return beside(
            [
                down(rows[:, :512], online_down[:, 1024:]),
                outward(rows[:, 512:], online_gate[1024:], online_up[1024:]),
            ]
        )

    left_parts = [left_terms(whole[576:])]
    right_parts = [right_terms(swapped[576:])]
    left_parts, right_parts = together(left_parts, right_parts)
    left_passing = halves_out(left_parts, along_z)
    right_passing = halves_out(right_parts, along_x)
    whole, swapped = after((whole, swapped), left_passing[0], right_passing[0])
    left_parts = jnp.split(left_terms(whole[:576]), 3, axis=0) + left_parts
    right_parts = jnp.split(right_terms(swapped[:576]), 3, axis=0) + right_parts
    left_passing, right_passing = together(left_passing, right_passing)
    left_out = with_passing(left_parts, left_passing)
    right_out = with_passing(right_parts, right_passing)
    left_out, right_out, late_rows, late_cot = together(left_out, right_out, rows_all, cot_all)
    left_far = [left_parts[0], along_z(left_out[0], -1), along_z(left_out[1], 1)]
    right_far = [right_parts[0], along_x(right_out[0], -1), along_x(right_out[1], 1)]

    on_hidden, d_gate, d_up = whole[:, :512], whole[:, 512:1024], whole[:, 1024:]
    grad_gate = (
        jnp.einsum("tk,tf->kf", late_rows, d_gate, preferred_element_type=F32) * SCALE_IN
    ).astype(BF)
    grad_up = (
        jnp.einsum("tk,tf->kf", late_rows, d_up, preferred_element_type=F32) * SCALE_IN
    ).astype(BF)
    grad_down = (
        jnp.einsum("tf,tk->fk", on_hidden, late_cot, preferred_element_type=F32) * SCALE_HID
    ).astype(BF)
    left_far, right_far, weight_outs = together(
        left_far, right_far, (grad_gate, grad_up, grad_down)
    )
    grad_gate, grad_up, grad_down = weight_outs

    def near(first, second, along):
        sums = split(beside([total_of(first), total_of(second)]))
        got = [along(part.astype(BF), -d) for part, d in list(zip(sums, FAR))[1:]]
        return [sums[0]] + got

    left_near = near(tg_left, left_far, along_x)
    right_near = near(tg_right, right_far, along_z)
    new_down = blend(online_down, after(target_down, left_near[1], right_near[1]))
    total = beside([total_of(left_near), total_of(right_near)])
    total = (total[:24] + shifted(total[24:].astype(BF), 0, 1, 0).astype(F32)).astype(BF)
    target_out, online_out, grad_in = (
        beside([total[:, 1024 * k : 1024 * k + 1024], total[:, 1024 * k + 3072 : 1024 * k + 4096]])
        for k in range(3)
    )
    return (
        online_out,
        target_out,
        grad_in,
        grad_gate,
        grad_up,
        grad_down,
        new_gate,
        new_up,
        new_down,
    )


def solution(mesh):
    tokens = P(("gy", "gz"), "gx")
    wide = P("gx", ("gy", "gz"))
    tall = P(("gy", "gz"), "gx")
    return jax.shard_map(
        on_device,
        mesh=mesh,
        in_specs=(tokens, wide, wide, tall, wide, wide, tall, tokens),
        out_specs=(tokens, tokens, tokens, wide, wide, tall, wide, wide, tall),
        check_vma=False,
    )
```

```python
import math

import jax
import jax.numpy as jnp
from jax import lax
from jax.sharding import PartitionSpec as P

D = 8192
FF = 16384
POLYAK = 0.05
BF = jnp.bfloat16
F32 = jnp.float32
SCALE_IN = 1.0 / math.sqrt(D)
SCALE_HID = 1.0 / math.sqrt(FF)
FAR = (0, 1, 3, 2)


def activate(pre_gate, pre_up):
    return (jax.nn.silu(pre_gate) * pre_up).astype(BF)


def hidden_grads(pre_gate, pre_up, hidden_grad):
    sigmoid_value = jax.nn.sigmoid(pre_gate)
    d_up = (hidden_grad * pre_gate * sigmoid_value).astype(BF)
    d_gate = (
        hidden_grad * pre_up * sigmoid_value * (1.0 + pre_gate * (1.0 - sigmoid_value))
    ).astype(BF)
    return (d_gate, d_up)


def blend(online, target):
    online_f = online.astype(F32)
    target_f = target.astype(F32)
    return (target_f + POLYAK * (online_f - target_f)).astype(BF)


def shifted(value, dz, dy, dx):
    pairs = []
    for z in range(4):
        for y in range(2):
            for x in range(4):
                to = ((z + dz) % 4 * 2 + (y + dy) % 2) * 4 + (x + dx) % 4
                pairs.append(((z * 2 + y) * 4 + x, to))
    return lax.ppermute(value, ("gy", "gz"), pairs)


def along_x(value, d):
    return shifted(value, 0, 0, d)


def along_z(value, d):
    return shifted(value, d, 0, 0)


def swap_zx(value):
    rows, columns = value.shape
    return value.reshape(4, 4, rows // 16, columns).swapaxes(0, 1).reshape(rows, columns)


def from_axis(value, along):
    return [value] + [along(value, d) for d in FAR[1:]]


def together(*values):
    return lax.optimization_barrier(values)


def passed_on(near, along):
    half = near[0].shape[0] // 2
    return [along(near[0][:half], 1), along(near[1][half:], 3)]


def halves_out(parts, along):
    far = parts[-1]
    half = far.shape[0] // 2
    return [along(far[:half], -1), along(far[half:], 1)]


def with_passing(parts, passing):
    _, back, ahead, _ = parts
    half = back.shape[0] // 2
    back = [(back[:half].astype(F32) + passing[0].astype(F32)).astype(BF), back[half:]]
    ahead = [ahead[:half], (ahead[half:].astype(F32) + passing[1].astype(F32)).astype(BF)]
    return [stack(back), stack(ahead)]


def to_axis(parts, along):
    return [parts[0]] + [along(part, -d) for part, d in list(zip(parts, FAR))[1:]]


def total_of(parts):
    total = parts[0].astype(F32)
    for part in parts[1:]:
        total = total + part.astype(F32)
    return total


def stack(parts):
    return jnp.concatenate(list(parts), axis=0)


def beside(parts):
    return jnp.concatenate(list(parts), axis=1)


def split(value):
    return jnp.split(value, 4, axis=0)


def other_core(value):
    return lax.ppermute(value, "gx", [(0, 1), (1, 0), (2, 3), (3, 2)])


def other_half(value):
    return lax.ppermute(value, "gx", [(0, 2), (1, 3), (2, 0), (3, 1)])


def after(value, *others):
    return lax.optimization_barrier((value,) + others)[0]


def on_device(
    block_in, online_gate, online_up, online_down, target_gate, target_up, target_down, cotangent
):
    core = lax.axis_index("gx") % 2

    def halves(value):
        half = value.shape[0] // 2
        keep = lax.dynamic_slice_in_dim(value, core * half, half, 0)
        send = lax.dynamic_slice_in_dim(value, (1 - core) * half, half, 0)
        return keep, send

    def both_halves(value):
        other = other_core(value)
        lower = jnp.where(core == 0, value, other)
        upper = jnp.where(core == 0, other, value)
        return stack([lower, upper])

    def project(rows, weight):
        return jnp.dot(rows, weight, preferred_element_type=F32) * SCALE_IN

    def back(rows):
        return jnp.einsum("tk,fk->tf", rows, online_down, preferred_element_type=F32) * SCALE_HID

    def down(hidden, weight):
        return (jnp.dot(hidden, weight, preferred_element_type=F32) * SCALE_HID).astype(BF)

    def outward(whole, gate, up):
        summed = jnp.einsum("tf,kf->tk", whole[:, :512], gate, preferred_element_type=F32)
        summed = summed + jnp.einsum("tf,kf->tk", whole[:, 512:], up, preferred_element_type=F32)
        return (summed * SCALE_IN).astype(BF)

    own = stack([block_in, cotangent])
    pair = shifted(own, 0, 1, 0)
    pair = beside([stack([own[:24], pair[:24]]), stack([own[24:], pair[24:]])])
    left = beside([pair[:, :1024], pair[:, 2048:3072]])
    right = beside([pair[:, 1024:2048], pair[:, 3072:]])
    left, right = together(left, right)
    left, right = stack(from_axis(left, along_x)), stack(from_axis(right, along_z))
    left_near = [along_z(left, 1), along_z(left, 3)]
    right_near = [along_x(right, 1), along_x(right, 3)]
    old_gate, old_up, old_down = after((target_gate, target_up, target_down), left, right)
    blends = (
        blend(online_gate, old_gate), blend(online_up, old_up), blend(online_down, old_down)
    )
    left_near, right_near, blends = together(left_near, right_near, blends)
    new_gate, new_up, new_down = blends
    left = [left] + left_near + passed_on(left_near, along_z)
    right = [right] + right_near + passed_on(right_near, along_x)
    left, right = stack(left), swap_zx(stack(right))
    rows_all = beside([left[:, :1024], right[:, :1024]])
    cot_all = beside([left[:, 1024:], right[:, 1024:]])

    rows_keep, rows_send = halves(rows_all)
    tg_send = beside([project(rows_send, w) for w in (target_gate, target_up)])
    tg_got = other_core(tg_send)
    tg_keep = beside([project(rows_keep, w) for w in (target_gate, target_up)])
    cot_late, rows_late = after((cot_all, rows_all), tg_keep)
    cot_keep, cot_send = halves(cot_late)
    rows_keep, rows_send = halves(rows_late)
    on_got = other_core(beside([project(rows_send, w) for w in (online_gate, online_up)]))
    back_got = other_core(back(cot_send))
    tg_chip = tg_keep + tg_got
    tg_wire, rows_keep, cot_keep = together(tg_chip.astype(BF), rows_keep, cot_keep)
    tg_there = other_half(tg_wire)
    on_chip = beside([project(rows_keep, w) for w in (online_gate, online_up)]) + on_got
    back_chip = back(cot_keep) + back_got
    wire = beside([on_chip, back_chip]).astype(BF)
    tg_there, wire = together(tg_there, wire)
    there = other_half(wire)

    pre = tg_chip + tg_there.astype(F32)
    hidden = both_halves(activate(pre[:, :512], pre[:, 512:]))
    tg_left = split(down(hidden, target_down[:, :1024]))
    tg_right = split(down(swap_zx(hidden), target_down[:, 1024:]))
    tg_left[1:3] = [along_z(tg_left[1], -1), along_z(tg_left[2], 1)]
    tg_right[1:3] = [along_x(tg_right[1], -1), along_x(tg_right[2], 1)]
    tg_left[3] = along_z(after(tg_left[3], tg_left[1]), 2)
    tg_right[3] = along_x(after(tg_right[3], tg_right[1]), 2)
    there, tg_left, tg_right = together(there, tg_left, tg_right)

    pre = on_chip + there[:, :1024].astype(F32)
    on_gate, on_up = pre[:, :512], pre[:, 512:]
    hidden_grad = back_chip + there[:, 1024:].astype(F32)
    d_gate, d_up = hidden_grads(on_gate, on_up, hidden_grad)
    whole = both_halves(beside([activate(on_gate, on_up), d_gate, d_up]))
    swapped = swap_zx(whole)

    def left_terms(rows):
        return beside(
            [
                down(rows[:, :512], online_down[:, :1024]),
                outward(rows[:, 512:], online_gate[:1024], online_up[:1024]),
            ]
        )

    def right_terms(rows):
        return beside(
            [
                down(rows[:, :512], online_down[:, 1024:]),
                outward(rows[:, 512:], online_gate[1024:], online_up[1024:]),
            ]
        )

    left_parts = [left_terms(whole[576:])]
    right_parts = [right_terms(swapped[576:])]
    left_parts, right_parts = together(left_parts, right_parts)
    left_passing = halves_out(left_parts, along_z)
    right_passing = halves_out(right_parts, along_x)
    whole, swapped = after((whole, swapped), left_passing[0], right_passing[0])
    left_parts = jnp.split(left_terms(whole[:576]), 3, axis=0) + left_parts
    right_parts = jnp.split(right_terms(swapped[:576]), 3, axis=0) + right_parts
    left_passing, right_passing = together(left_passing, right_passing)
    left_out = with_passing(left_parts, left_passing)
    right_out = with_passing(right_parts, right_passing)
    left_out, right_out, late_rows, late_cot = together(left_out, right_out, rows_all, cot_all)
    left_far = [left_parts[0], along_z(left_out[0], -1), along_z(left_out[1], 1)]
    right_far = [right_parts[0], along_x(right_out[0], -1), along_x(right_out[1], 1)]

    on_hidden, d_gate, d_up = whole[:, :512], whole[:, 512:1024], whole[:, 1024:]
    grad_gate = (
        jnp.einsum("tk,tf->kf", late_rows, d_gate, preferred_element_type=F32) * SCALE_IN
    ).astype(BF)
    grad_up = (
        jnp.einsum("tk,tf->kf", late_rows, d_up, preferred_element_type=F32) * SCALE_IN
    ).astype(BF)
    grad_down = (
        jnp.einsum("tf,tk->fk", on_hidden, late_cot, preferred_element_type=F32) * SCALE_HID
    ).astype(BF)
    left_far, right_far, weight_outs = together(
        left_far, right_far, (grad_gate, grad_up, grad_down)
    )
    grad_gate, grad_up, grad_down = weight_outs

    def near(first, second, along):
        sums = split(beside([total_of(first), total_of(second)]))
        got = [along(part.astype(BF), -d) for part, d in list(zip(sums, FAR))[1:]]
        return [sums[0]] + got

    left_near = near(tg_left, left_far, along_x)
    right_near = near(tg_right, right_far, along_z)
    sides = []
    for parts in (left_near, right_near):
        total = total_of(parts)
        sides.append((total[:24], shifted(total[24:].astype(BF), 0, 1, 0)))
    target_out, online_out, grad_in = (
        beside(
            [
                (own[:, span] + got[:, span].astype(F32)).astype(BF)
                for own, got in sides
            ]
        )
        for span in (slice(0, 1024), slice(1024, 2048), slice(2048, 3072))
    )
    return (
        online_out,
        target_out,
        grad_in,
        grad_gate,
        grad_up,
        grad_down,
        new_gate,
        new_up,
        new_down,
    )


def solution(mesh):
    tokens = P(("gy", "gz"), "gx")
    wide = P("gx", ("gy", "gz"))
    tall = P(("gy", "gz"), "gx")
    return jax.shard_map(
        on_device,
        mesh=mesh,
        in_specs=(tokens, wide, wide, tall, wide, wide, tall, tokens),
        out_specs=(tokens, tokens, tokens, wide, wide, tall, wide, wide, tall),
        check_vma=False,
    )
```

```python
import math

import jax
import jax.numpy as jnp
from jax import lax
from jax.sharding import PartitionSpec as P

D = 8192
FF = 16384
POLYAK = 0.05
BF = jnp.bfloat16
F32 = jnp.float32
SCALE_IN = 1.0 / math.sqrt(D)
SCALE_HID = 1.0 / math.sqrt(FF)
FAR = (0, 1, 3, 2)


def activate(pre_gate, pre_up):
    return (jax.nn.silu(pre_gate) * pre_up).astype(BF)


def hidden_grads(pre_gate, pre_up, hidden_grad):
    sigmoid_value = jax.nn.sigmoid(pre_gate)
    d_up = (hidden_grad * pre_gate * sigmoid_value).astype(BF)
    d_gate = (
        hidden_grad * pre_up * sigmoid_value * (1.0 + pre_gate * (1.0 - sigmoid_value))
    ).astype(BF)
    return (d_gate, d_up)


def blend(online, target):
    online_f = online.astype(F32)
    target_f = target.astype(F32)
    return (target_f + POLYAK * (online_f - target_f)).astype(BF)


def shifted(value, dz, dy, dx):
    pairs = []
    for z in range(4):
        for y in range(2):
            for x in range(4):
                to = ((z + dz) % 4 * 2 + (y + dy) % 2) * 4 + (x + dx) % 4
                pairs.append(((z * 2 + y) * 4 + x, to))
    return lax.ppermute(value, ("gy", "gz"), pairs)


def along_x(value, d):
    return shifted(value, 0, 0, d)


def along_z(value, d):
    return shifted(value, d, 0, 0)


def swap_zx(value):
    rows, columns = value.shape
    return value.reshape(4, 4, rows // 16, columns).swapaxes(0, 1).reshape(rows, columns)


def from_axis(value, along):
    return [value] + [along(value, d) for d in FAR[1:]]


def together(*values):
    return lax.optimization_barrier(values)


def passed_on(near, along):
    half = near[0].shape[0] // 2
    return [along(near[0][:half], 1), along(near[1][half:], 3)]


def halves_out(parts, along):
    far = parts[-1]
    half = far.shape[0] // 2
    return [along(far[:half], -1), along(far[half:], 1)]


def with_passing(parts, passing):
    _, back, ahead, _ = parts
    half = back.shape[0] // 2
    back = [(back[:half].astype(F32) + passing[0].astype(F32)).astype(BF), back[half:]]
    ahead = [ahead[:half], (ahead[half:].astype(F32) + passing[1].astype(F32)).astype(BF)]
    return [stack(back), stack(ahead)]


def to_axis(parts, along):
    return [parts[0]] + [along(part, -d) for part, d in list(zip(parts, FAR))[1:]]


def total_of(parts):
    total = parts[0].astype(F32)
    for part in parts[1:]:
        total = total + part.astype(F32)
    return total


def stack(parts):
    return jnp.concatenate(list(parts), axis=0)


def beside(parts):
    return jnp.concatenate(list(parts), axis=1)


def split(value):
    return jnp.split(value, 4, axis=0)


def other_core(value):
    return lax.ppermute(value, "gx", [(0, 1), (1, 0), (2, 3), (3, 2)])


def other_half(value):
    return lax.ppermute(value, "gx", [(0, 2), (1, 3), (2, 0), (3, 1)])


def after(value, *others):
    return lax.optimization_barrier((value,) + others)[0]


def on_device(
    block_in, online_gate, online_up, online_down, target_gate, target_up, target_down, cotangent
):
    core = lax.axis_index("gx") % 2

    def halves(value):
        half = value.shape[0] // 2
        keep = lax.dynamic_slice_in_dim(value, core * half, half, 0)
        send = lax.dynamic_slice_in_dim(value, (1 - core) * half, half, 0)
        return keep, send

    def both_halves(value):
        other = other_core(value)
        lower = jnp.where(core == 0, value, other)
        upper = jnp.where(core == 0, other, value)
        return stack([lower, upper])

    def project(rows, weight):
        return jnp.dot(rows, weight, preferred_element_type=F32) * SCALE_IN

    def back(rows):
        return jnp.einsum("tk,fk->tf", rows, online_down, preferred_element_type=F32) * SCALE_HID

    def down(hidden, weight):
        return (jnp.dot(hidden, weight, preferred_element_type=F32) * SCALE_HID).astype(BF)

    def outward(whole, gate, up):
        summed = jnp.einsum("tf,kf->tk", whole[:, :512], gate, preferred_element_type=F32)
        summed = summed + jnp.einsum("tf,kf->tk", whole[:, 512:], up, preferred_element_type=F32)
        return (summed * SCALE_IN).astype(BF)

    own = stack([block_in, cotangent])
    pair = shifted(own, 0, 1, 0)
    pair = beside([stack([own[:24], pair[:24]]), stack([own[24:], pair[24:]])])
    left = beside([pair[:, :1024], pair[:, 2048:3072]])
    right = beside([pair[:, 1024:2048], pair[:, 3072:]])
    left, right = together(left, right)
    left, right = stack(from_axis(left, along_x)), stack(from_axis(right, along_z))
    left_near = [along_z(left, 1), along_z(left, 3)]
    right_near = [along_x(right, 1), along_x(right, 3)]
    old_gate, old_up, old_down = after((target_gate, target_up, target_down), left, right)
    blends = (
        blend(online_gate, old_gate), blend(online_up, old_up), blend(online_down, old_down)
    )
    left_near, right_near, blends = together(left_near, right_near, blends)
    new_gate, new_up, new_down = blends
    left = [left] + left_near + passed_on(left_near, along_z)
    right = [right] + right_near + passed_on(right_near, along_x)
    left, right = stack(left), swap_zx(stack(right))
    rows_all = beside([left[:, :1024], right[:, :1024]])
    cot_all = beside([left[:, 1024:], right[:, 1024:]])

    rows_keep, rows_send = halves(rows_all)
    tg_send = beside([project(rows_send, w) for w in (target_gate, target_up)])
    tg_got = other_core(tg_send)
    tg_keep = beside([project(rows_keep, w) for w in (target_gate, target_up)])
    cot_late, rows_late = after((cot_all, rows_all), tg_keep)
    cot_keep, cot_send = halves(cot_late)
    rows_keep, rows_send = halves(rows_late)
    on_got = other_core(beside([project(rows_send, w) for w in (online_gate, online_up)]))
    back_got = other_core(back(cot_send))
    tg_chip = tg_keep + tg_got
    tg_wire, rows_keep, cot_keep = together(tg_chip.astype(BF), rows_keep, cot_keep)
    tg_there = other_half(tg_wire)
    on_chip = beside([project(rows_keep, w) for w in (online_gate, online_up)]) + on_got
    back_chip = back(cot_keep) + back_got
    wire = beside([on_chip, back_chip]).astype(BF)
    tg_there, wire = together(tg_there, wire)
    there = other_half(wire)

    pre = tg_chip + tg_there.astype(F32)
    hidden = both_halves(activate(pre[:, :512], pre[:, 512:]))
    tg_left = split(down(hidden, target_down[:, :1024]))
    tg_right = split(down(swap_zx(hidden), target_down[:, 1024:]))
    tg_left[1:3] = [along_z(tg_left[1], -1), along_z(tg_left[2], 1)]
    tg_right[1:3] = [along_x(tg_right[1], -1), along_x(tg_right[2], 1)]
    tg_left[3] = along_z(after(tg_left[3], tg_left[1]), 2)
    tg_right[3] = along_x(after(tg_right[3], tg_right[1]), 2)
    there, tg_left, tg_right = together(there, tg_left, tg_right)

    pre = on_chip + there[:, :1024].astype(F32)
    on_gate, on_up = pre[:, :512], pre[:, 512:]
    hidden_grad = back_chip + there[:, 1024:].astype(F32)
    d_gate, d_up = hidden_grads(on_gate, on_up, hidden_grad)
    whole = both_halves(beside([activate(on_gate, on_up), d_gate, d_up]))
    swapped = swap_zx(whole)

    def left_terms(rows):
        return beside(
            [
                down(rows[:, :512], online_down[:, :1024]),
                outward(rows[:, 512:], online_gate[:1024], online_up[:1024]),
            ]
        )

    def right_terms(rows):
        return beside(
            [
                down(rows[:, :512], online_down[:, 1024:]),
                outward(rows[:, 512:], online_gate[1024:], online_up[1024:]),
            ]
        )

    left_parts = [left_terms(whole[576:])]
    right_parts = [right_terms(swapped[576:])]
    left_parts, right_parts = together(left_parts, right_parts)
    left_passing = halves_out(left_parts, along_z)
    right_passing = halves_out(right_parts, along_x)
    whole, swapped = after((whole, swapped), left_passing[0], right_passing[0])
    left_parts = jnp.split(left_terms(whole[:576]), 3, axis=0) + left_parts
    right_parts = jnp.split(right_terms(swapped[:576]), 3, axis=0) + right_parts
    left_out = with_passing(left_parts, left_passing)
    right_out = with_passing(right_parts, right_passing)
    late_rows, late_cot = after((rows_all, cot_all), left_out, right_out)
    left_far = [left_parts[0], along_z(left_out[0], -1), along_z(left_out[1], 1)]
    right_far = [right_parts[0], along_x(right_out[0], -1), along_x(right_out[1], 1)]

    on_hidden, d_gate, d_up = whole[:, :512], whole[:, 512:1024], whole[:, 1024:]
    grad_gate = (
        jnp.einsum("tk,tf->kf", late_rows, d_gate, preferred_element_type=F32) * SCALE_IN
    ).astype(BF)
    grad_up = (
        jnp.einsum("tk,tf->kf", late_rows, d_up, preferred_element_type=F32) * SCALE_IN
    ).astype(BF)
    grad_down = (
        jnp.einsum("tf,tk->fk", on_hidden, late_cot, preferred_element_type=F32) * SCALE_HID
    ).astype(BF)
    left_far, right_far, weight_outs = together(
        left_far, right_far, (grad_gate, grad_up, grad_down)
    )
    grad_gate, grad_up, grad_down = weight_outs

    def near(first, second, along):
        sums = split(beside([total_of(first), total_of(second)]))
        got = [along(part.astype(BF), -d) for part, d in list(zip(sums, FAR))[1:]]
        return [sums[0]] + got

    left_near = near(tg_left, left_far, along_x)
    right_near = near(tg_right, right_far, along_z)
    sides = []
    for parts in (left_near, right_near):
        total = total_of(parts)
        sides.append((total[:24], shifted(total[24:].astype(BF), 0, 1, 0)))
    target_out, online_out, grad_in = (
        beside(
            [
                (own[:, span] + got[:, span].astype(F32)).astype(BF)
                for own, got in sides
            ]
        )
        for span in (slice(0, 1024), slice(1024, 2048), slice(2048, 3072))
    )
    return (
        online_out,
        target_out,
        grad_in,
        grad_gate,
        grad_up,
        grad_down,
        new_gate,
        new_up,
        new_down,
    )


def solution(mesh):
    tokens = P(("gy", "gz"), "gx")
    wide = P("gx", ("gy", "gz"))
    tall = P(("gy", "gz"), "gx")
    return jax.shard_map(
        on_device,
        mesh=mesh,
        in_specs=(tokens, wide, wide, tall, wide, wide, tall, tokens),
        out_specs=(tokens, tokens, tokens, wide, wide, tall, wide, wide, tall),
        check_vma=False,
    )
```
